512 devices in a mesh: grp: 16 (over x, y), dev: 32 (over z, core).
Axes of the slice: x: 4, y: 4, z: 16, core: 2. Of those that a mesh axis runs over, the one named last changes fastest.
Arguments:
- records: bfloat16 [131072, 128], P('grp', 'dev')
- dropout: int32 [131072, 128], P('grp', 'dev'), may hold values 0 or 1
- counts: int32 [512], P(('grp', 'dev')), may hold values from 128 to 256, as said below
Outputs:
- upper: float32 [512, 512], replicated
- basis: bfloat16 [131072, 512], P(('grp', 'dev'))
The draws below stay inside these ranges and needn't reach their ends.
Inputs may be any that keep to these rules, and one draw needn't show every extreme that they name: `counts`: at least one time shard has all 256 rows valid.
All inputs are finite; a program needn't handle non-finite values. No bound on the sum of `dropout` on one device may be relied on, other than what follows from the above.
Results may differ from the reference program's by a relative error of at most 0.0012.
Values may be sent and summed in bfloat16 or wider, within the bound.
No kernel may reach another device: no remote copies, remote signals or barrier semaphores. Data moves between devices by JAX's collectives and lax.ppermute only.
A program may use at most 128 MiB of HBM per device.

```python
import jax
import jax.numpy as jnp
from jax import lax

CHANNELS = 128
LAGS = 4
ROWS_DEV = 256
COLS = 512
SHARDS = 512
TOTAL = 131072


def draw_records(key, part):
    keys = jax.random.split(jax.random.fold_in(key, 11), 8)
    amplitude = jnp.exp(jax.random.uniform(keys[0], (SHARDS,), jnp.float32, jnp.log(0.3), jnp.log(3.0)))
    channel_gain = jnp.exp(jax.random.uniform(keys[1], (CHANNELS,), jnp.float32, jnp.log(0.3), jnp.log(3.0)))
    mode_rate = jax.random.randint(keys[2], (24,), 40, 2000, jnp.int32)
    mode_phase = jax.random.uniform(keys[3], (24,), jnp.float32, -jnp.pi, jnp.pi)
    mode_weight = jnp.exp(jax.random.uniform(keys[4], (24,), jnp.float32, jnp.log(0.5), jnp.log(2.0)))
    mode_shape = jax.random.normal(keys[5], (24, CHANNELS), jnp.float32)
    shard_weight = jax.random.uniform(keys[6], (SHARDS, 24), jnp.float32, 0.5, 1.5)
    times = jnp.arange(SHARDS * ROWS_DEV, dtype=jnp.int32).reshape(SHARDS, ROWS_DEV)
    folded = times % 40000
    noise = jnp.clip(jax.random.normal(keys[7], (SHARDS, ROWS_DEV, CHANNELS), jnp.float32), -6.0, 6.0)
    level_base = 1.5 * jnp.sqrt(2.0 / 24.0)
    modal = jnp.zeros((SHARDS, ROWS_DEV, CHANNELS), jnp.float32)
    for number in range(24):
        cycle = (folded * mode_rate[number] % 40000).astype(jnp.float32)
        phase = cycle * (2.0 * jnp.pi / 40000.0) + mode_phase[number]
        level = level_base * mode_weight[number] * shard_weight[:, number][:, None]
        modal = modal + (level * jnp.cos(phase))[:, :, None] * mode_shape[number][None, None, :]
    values = (modal + noise) * amplitude[:, None, None] * channel_gain[None, None, :]
    return values.reshape(SHARDS * ROWS_DEV, CHANNELS).astype(jnp.bfloat16)


def draw_counts(key, part):
    key_vals, key_full = jax.random.split(jax.random.fold_in(key, 7))
    values = jax.random.randint(key_vals, (SHARDS,), ROWS_DEV // 2, ROWS_DEV + 1, jnp.int32)
    fullest = jax.random.randint(key_full, (), 0, SHARDS, jnp.int32)
    return jnp.where(jnp.arange(SHARDS, dtype=jnp.int32) == fullest, ROWS_DEV, values).astype(jnp.int32)


def set_ends(entries, key, least, top_value):
    shape = entries.shape
    index_at = [jax.random.randint(jax.random.fold_in(key, axis), (), 0, shape[axis]) for axis in range(len(shape))]
    entries = entries.at[tuple(index_at)].set(least)
    longest = shape.index(max(shape))
    index_at[longest] = (index_at[longest] + 1) % shape[longest]
    return entries.at[tuple(index_at)].set(top_value)


def setup_inputs(seed: int = 0) -> dict:
    splits = jax.random.split(jax.random.key(seed), 4)
    records = draw_records(jax.random.fold_in(splits[3], 71), 0)
    dropout = set_ends((jax.random.randint(splits[1], (TOTAL, CHANNELS), 0, 10) < 9).astype(jnp.int32), jax.random.fold_in(splits[1], 1), 0, 1)
    counts = draw_counts(jax.random.fold_in(splits[3], 71), 0)
    return {"records": records, "dropout": dropout, "counts": counts}


def shard_hankel(padded, counts, shard):
    start = (shard * ROWS_DEV).astype(jnp.int32)
    window = lax.dynamic_slice_in_dim(padded, start, ROWS_DEV + LAGS - 1, 0)
    hankel = jnp.concatenate([window[k:k + ROWS_DEV] for k in range(LAGS)], axis=1)
    valid = jnp.arange(ROWS_DEV, dtype=jnp.int32) >= ROWS_DEV - counts[shard]
    return jnp.where(valid[:, None], hankel, jnp.zeros_like(hankel))

def reference(records, dropout, counts):
    signal = (records.astype(jnp.float32) * dropout.astype(jnp.float32)).astype(jnp.bfloat16)
    padded = jnp.concatenate([signal, jnp.zeros((LAGS - 1, CHANNELS), jnp.bfloat16)], axis=0)
    shards = jnp.arange(SHARDS, dtype=jnp.int32)

    def accumulate(total, shard):
        hankel = shard_hankel(padded, counts, shard)
        term = lax.dot_general(hankel.astype(jnp.float32), hankel.astype(jnp.float32), (((0,), (0,)), ((), ())), preferred_element_type=jnp.float32)
        return (total + term, None)
    gram, _ = lax.scan(accumulate, jnp.zeros((COLS, COLS), jnp.float32), shards)
    lower = jnp.linalg.cholesky(gram / TOTAL)
    upper = jnp.transpose(lower)
    identity = jnp.eye(COLS, dtype=upper.dtype)
    inverse = lax.linalg.triangular_solve(upper, identity, left_side=True, lower=False)

    def project(shard):
        hankel = shard_hankel(padded, counts, shard).astype(jnp.float32)
        return jnp.dot(hankel, inverse, precision=lax.Precision.HIGHEST).astype(jnp.bfloat16)
    basis = lax.map(project, shards).reshape(TOTAL, COLS)
    return (upper, basis)
```

```python
import jax
import jax.numpy as jnp
from jax import lax
from jax.experimental import pallas as pl
from jax.experimental.pallas import tpu as pltpu
from jax.sharding import PartitionSpec as P

f32, bf16 = jnp.float32, jnp.bfloat16

LAGS = 4
CHANNELS = 128
ROWS = 256
COLS = 512
TOTAL = 131072
GROUPS = 16
WINDOW = 640
PAIRS = [(i, j) for i in range(LAGS) for j in range(i, LAGS)]
HALF = 64
PACKED = HALF * len(PAIRS)
SLICE = PACKED // GROUPS

PARAMS = pltpu.CompilerParams(vmem_limit_bytes=48 * 2**20)
SMEM = pl.BlockSpec(memory_space=pltpu.SMEM)
VMEM = pl.BlockSpec(memory_space=pltpu.VMEM)


def split(x):
    high = x.astype(bf16)
    return high, (x - high.astype(f32)).astype(bf16)


def dot_tn(left, right):
    return lax.dot_general(left, right, (((0,), (0,)), ((), ())), preferred_element_type=f32)


def dot_nt(left, right):
    return lax.dot_general(left, right, (((1,), (1,)), ((), ())), preferred_element_type=f32)


def dot_nn(left, right):
    return jnp.dot(left, right, preferred_element_type=f32)


def triple(x, order, axis):
    high, low = split(x)
    return jnp.concatenate([low if c == "l" else high for c in order], axis=axis)


def pack_kernel(count, records, dropout, head, out):
    signal = (records[...].astype(f32) * dropout[...].astype(f32)).astype(bf16)
    lane = lax.broadcasted_iota(jnp.int32, (4, 128), 1)
    counted = jnp.full((4, 128), count[0], jnp.int32).astype(f32)
    for z in range(16):
        behind = signal[:, 512 * z + 512 : 512 * z + 640] if z < 15 else head[...]
        behind = jnp.where(lane == 127, counted, behind.astype(f32)).astype(bf16)
        for core in range(2):
            out[2 * z + core, :, 0:512] = signal[:, 512 * z : 512 * z + 512]
            out[2 * z + core, :, 512:640] = behind


def gram_kernel(place, series, packed, hankel, lagged):
    z, core = place[0], place[1]
    samples = series[...].astype(f32)
    source = lax.broadcasted_iota(jnp.int32, (CHANNELS, 1), 0)
    tail = samples[:, WINDOW - 1 : WINDOW]
    time = lax.broadcasted_iota(jnp.int32, (1, 512), 1)
    counts = [
        jnp.sum(jnp.where(source == 8 * z + 4 * e, tail, 0.0), axis=0, keepdims=True) for e in range(2)
    ]
    least = jnp.where(time < ROWS, ROWS - counts[0], 2 * ROWS - counts[1])
    valid = time.astype(f32) >= least
    for i in range(LAGS):
        moved = samples if i == 0 else pltpu.roll(samples, WINDOW - i, 1)
        lagged[CHANNELS * i : CHANNELS * (i + 1), :] = jnp.where(valid, moved[:, :512], 0.0).astype(bf16)
    every = lagged[...]
    mine = jnp.concatenate(
        [lagged[pl.ds(pl.multiple_of(CHANNELS * i + HALF * core, HALF), HALF), :] for i in range(LAGS)], axis=0
    )
    gram = dot_nt(mine, every)
    for b, (i, j) in enumerate(PAIRS):
        packed[HALF * b : HALF * (b + 1), :] = gram[HALF * i : HALF * (i + 1), CHANNELS * j : CHANNELS * (j + 1)]
    own = lagged[:, pl.ds(pl.multiple_of(ROWS * core, ROWS), ROWS)]
    hankel[...] = jnp.transpose(own.astype(f32)).astype(bf16)


def sum_kernel(parts, out):
    total = parts[0]
    for s in range(1, GROUPS):
        total = total + parts[s]
    for s in range(GROUPS):
        out[s] = total


def pivots(work, start):
    lanes = (8, 128)
    sub = lax.broadcasted_iota(jnp.int32, lanes, 0)
    parts = [work[start : start + 8, 0:128], work[start : start + 8, 128:256]]
    cols = [jnp.broadcast_to(parts[0][:, start + i : start + i + 1], lanes) for i in range(8)]
    scale = jnp.ones(lanes, f32)
    for k in range(8):
        pivot = jnp.broadcast_to(cols[k][k : k + 1, :], lanes)
        factor = jnp.where(sub > k, cols[k] * (1.0 / pivot), 0.0)
        scale = jnp.where(sub == k, lax.rsqrt(pivot), scale)
        for i in range(k + 1, 8):
            cols[i] = cols[i] - factor * jnp.broadcast_to(cols[i][k : k + 1, :], lanes)
        parts = [v - factor * jnp.broadcast_to(v[k : k + 1, :], lanes) for v in parts]
    return [v * scale for v in parts]


def factor_diag(work, rows):
    for start in range(0, 128, 8):
        done = jnp.concatenate(pivots(work, start), axis=1)
        rows[start : start + 8, :] = done
        if start < 120:
            high = done.astype(bf16).astype(f32)
            low = done - high
            left = jnp.concatenate([high[:, :128], high[:, :128], low[:, :128]], axis=0).astype(bf16)
            right = jnp.concatenate([high, low, high], axis=0).astype(bf16)
            change = dot_tn(left, right)
            work[start + 8 : 128, :] = work[start + 8 : 128, :] - change[start + 8 : 128, :]


def factor_kernel(place, own, other, hankel, upper, basis, gram, work, rows, behind):
    core = place[1]
    for b, (i, j) in enumerate(PAIRS):
        block = pl.ds(HALF * b, HALF)
        cols = pl.ds(CHANNELS * j, CHANNELS)
        gram[pl.ds(pl.multiple_of(CHANNELS * i + HALF * core, HALF), HALF), cols] = own[block, :] * (1.0 / TOTAL)
        gram[pl.ds(pl.multiple_of(CHANNELS * i + HALF * (1 - core), HALF), HALF), cols] = other[block, :] * (1.0 / TOTAL)
    above = lax.broadcasted_iota(jnp.int32, (128, 128), 1)
    below = lax.broadcasted_iota(jnp.int32, (128, 128), 0)
    for p in range(4):
        lo, hi = 128 * p, 128 * p + 128
        work[:, 0:128] = gram[lo:hi, lo:hi]
        work[:, 128:256] = (above == below).astype(f32)
        factor_diag(work, rows)
        upper[lo:hi, lo:hi] = jnp.where(above >= below, rows[:, 0:128], 0.0)
        if p > 0:
            upper[lo:hi, 0:lo] = jnp.zeros((128, lo), f32)
        inverse = jnp.where(above <= below, rows[:, 128:256], 0.0)
        stacked = triple(inverse, "hhl", 1)
        if p > 0:
            left = dot_nn(stacked, triple(behind[lo:hi, 0:lo], "hlh", 0))
            full = jnp.concatenate([left, inverse], axis=1)
        else:
            full = inverse
        if p < 3:
            right = dot_nn(stacked, triple(gram[lo:hi, hi:512], "hlh", 0))
            upper[lo:hi, hi:512] = right
            first, second = triple(right, "hhl", 0), triple(right, "hlh", 0)
            for q in range(p + 1, 4):
                a = 128 * (q - p - 1)
                at = slice(128 * q, 128 * q + 128), slice(128 * q, 512)
                gram[at] = gram[at] - dot_tn(first[:, a : a + 128], second[:, a:])
            change = dot_tn(first, triple(full, "hlh", 0))
            if p > 0:
                behind[hi:512, 0:lo] = behind[hi:512, 0:lo] - change[:, 0:lo]
            behind[hi:512, lo:hi] = -change[:, lo:hi]
        high, low = split(full)
        basis[:, lo:hi] = (dot_nt(hankel[:, 0:hi], high) + dot_nt(hankel[:, 0:hi], low)).astype(bf16)


def shards(records, dropout, counts):
    z = lax.axis_index("dev") // 2
    core = lax.axis_index("dev") % 2
    place = jnp.stack([z, core]).astype(jnp.int32)
    recs, drops = records.T, dropout.T
    head = (recs[:, :128].astype(f32) * drops[:, :128].astype(f32)).astype(bf16)
    head = lax.ppermute(head, "grp", [(g, g - 1) for g in range(1, GROUPS)])
    sent = pl.pallas_call(
        pack_kernel,
        out_shape=jax.ShapeDtypeStruct((32, 4, WINDOW), bf16),
        in_specs=[SMEM, VMEM, VMEM, VMEM],
        compiler_params=PARAMS,
        name="pack",
    )(counts, recs, drops, head)
    series = lax.all_to_all(sent, "dev", 0, 0, tiled=True).reshape(CHANNELS, WINDOW)
    packed, hankel = pl.pallas_call(
        gram_kernel,
        out_shape=(jax.ShapeDtypeStruct((PACKED, 128), f32), jax.ShapeDtypeStruct((ROWS, COLS), bf16)),
        in_specs=[SMEM, VMEM],
        scratch_shapes=[pltpu.VMEM((COLS, 512), bf16)],
        compiler_params=PARAMS,
        name="partial_gram",
    )(place, series)
    add = pl.pallas_call(
        sum_kernel,
        out_shape=jax.ShapeDtypeStruct((GROUPS, SLICE, 128), f32),
        compiler_params=PARAMS,
        name="add_up",
    )
    along_z = [[2 * a + c for a in range(16)] for c in range(2)]
    parts = lax.all_to_all(packed.reshape(GROUPS, SLICE, 128), "grp", 0, 0, tiled=True)
    parts = lax.all_to_all(add(parts), "dev", 0, 0, axis_index_groups=along_z, tiled=True)
    own = lax.all_to_all(add(parts), "grp", 0, 0, tiled=True).reshape(PACKED, 128)
    other = lax.ppermute(own, "dev", [(d, d ^ 1) for d in range(32)])
    upper, basis = pl.pallas_call(
        factor_kernel,
        out_shape=(jax.ShapeDtypeStruct((COLS, COLS), f32), jax.ShapeDtypeStruct((ROWS, COLS), bf16)),
        in_specs=[SMEM, VMEM, VMEM, VMEM],
        scratch_shapes=[
            pltpu.VMEM((COLS, COLS), f32),
            pltpu.VMEM((128, 256), f32),
            pltpu.VMEM((128, 256), f32),
            pltpu.VMEM((COLS, 384), f32),
        ],
        compiler_params=PARAMS,
        name="factor",
    )(place, own, other, hankel)
    return (upper, basis)


def solution(mesh):
    in_specs = (P("grp", "dev"), P("grp", "dev"), P(("grp", "dev")))
    out_specs = (P(), P(("grp", "dev"), None))
    return jax.shard_map(shards, mesh=mesh, in_specs=in_specs, out_specs=out_specs, check_vma=False)
```

```python
import jax
import jax.numpy as jnp
from jax import lax
from jax.experimental import pallas as pl
from jax.experimental.pallas import tpu as pltpu
from jax.sharding import Mesh
from jax.sharding import PartitionSpec as P

f32, bf16 = jnp.float32, jnp.bfloat16

LAGS = 4
CHANNELS = 128
ROWS = 256
COLS = 512
TOTAL = 131072
GROUPS = 16
OWNERS = 32
PLANES = 8
WINDOW = 640
PAIRS = [(i, j) for i in range(LAGS) for j in range(i, LAGS)]
HALF = 64
SLICE = HALF * len(PAIRS) // OWNERS
STEP = 32

PARAMS = pltpu.CompilerParams(vmem_limit_bytes=48 * 2**20)
SMEM = pl.BlockSpec(memory_space=pltpu.SMEM)
VMEM = pl.BlockSpec(memory_space=pltpu.VMEM)
ANY = pl.BlockSpec(memory_space=pl.ANY)


def split(x):
    high = x.astype(bf16)
    return high, (x - high.astype(f32)).astype(bf16)


def dot_tn(left, right):
    return lax.dot_general(left, right, (((0,), (0,)), ((), ())), preferred_element_type=f32)


def dot_nt(left, right):
    return lax.dot_general(left, right, (((1,), (1,)), ((), ())), preferred_element_type=f32)


def dot_nn(left, right):
    return jnp.dot(left, right, preferred_element_type=f32)


def triple(x, order, axis):
    high, low = split(x)
    return jnp.concatenate([low if c == "l" else high for c in order], axis=axis)


def pack_kernel(place, count, records, dropout, out):
    signal = (records[...].astype(f32) * dropout[...].astype(f32)).astype(bf16)
    lane = lax.broadcasted_iota(jnp.int32, (4, 128), 1)
    counted = jnp.full((4, 128), count[0], jnp.int32).astype(f32)
    for z in range(16):
        behind = signal[:, 512 * z + 512 : 512 * z + 640] if z < 15 else jnp.zeros((4, 128), bf16)
        behind = jnp.where(lane == 127, counted, behind.astype(f32)).astype(bf16)
        for core in range(2):
            out[2 * z + core, :, 0:512] = signal[:, 512 * z : 512 * z + 512]
            out[2 * z + core, :, 512:640] = behind


def head_kernel(count, head, packed, out, behind, sem):
    lane = lax.broadcasted_iota(jnp.int32, (4, 128), 1)
    counted = jnp.full((4, 128), count[0], jnp.int32).astype(f32)
    value = jnp.where(lane == 127, counted, head[...].astype(f32)).astype(bf16)
    behind[0] = value
    behind[1] = value
    copy = pltpu.make_async_copy(behind, out.at[30:32, :, 512:640], sem)
    copy.start()
    copy.wait()


def gram_kernel(place, series, packed, hankel, lagged):
    z, core = place[0], place[1]
    samples = series[...].astype(f32)
    source = lax.broadcasted_iota(jnp.int32, (CHANNELS, 1), 0)
    tail = samples[:, WINDOW - 1 : WINDOW]
    time = lax.broadcasted_iota(jnp.int32, (1, 512), 1)
    counts = [
        jnp.sum(jnp.where(source == 8 * z + 4 * e, tail, 0.0), axis=0, keepdims=True) for e in range(2)
    ]
    least = jnp.where(time < ROWS, ROWS - counts[0], 2 * ROWS - counts[1])
    valid = time.astype(f32) >= least
    for i in range(LAGS):
        moved = samples if i == 0 else pltpu.roll(samples, WINDOW - i, 1)
        lagged[CHANNELS * i : CHANNELS * (i + 1), :] = jnp.where(valid, moved[:, :512], 0.0).astype(bf16)
    every = lagged[...]
    mine = jnp.concatenate(
        [lagged[pl.ds(pl.multiple_of(CHANNELS * i + HALF * core, HALF), HALF), :] for i in range(LAGS)], axis=0
    )
    gram = dot_nt(mine, every)

    def tile(t):
        (i, j), s = PAIRS[t // 8], t % 8
        return gram[HALF * i + 8 * s : HALF * i + 8 * s + 8, CHANNELS * j : CHANNELS * (j + 1)]

    for m in range(OWNERS):
        packed[m, 0:8, :] = tile(2 * m)
        packed[m, 8:16, :] = tile(2 * m + 1)
        packed[m, 16:20, :] = tile(2 * OWNERS + m // 2)[4 * (m % 2) : 4 * (m % 2) + 4, :]
    own = lagged[:, pl.ds(pl.multiple_of(ROWS * core, ROWS), ROWS)]
    hankel[...] = jnp.transpose(own.astype(f32)).astype(bf16)


def sum_kernel(parts, out):
    total = parts[0]
    for s in range(1, parts.shape[0]):
        total = total + parts[s]
    for s in range(out.shape[0]):
        out[s] = total


def add_up(parts, copies):
    return pl.pallas_call(
        sum_kernel,
        out_shape=jax.ShapeDtypeStruct((copies, SLICE, 128), f32),
        compiler_params=PARAMS,
        name="add_up",
    )(parts)


def spread(value, sublane):
    return jnp.broadcast_to(value[sublane : sublane + 1, :], (8, 128))


def pivots(work, start):
    sub = lax.broadcasted_iota(jnp.int32, (8, 128), 0)
    blocks = STEP // 8
    parts = [
        [work[start + 8 * b : start + 8 * b + 8, 128 * t : 128 * t + 128] for t in range(2)] for b in range(blocks)
    ]
    cols = [
        {b: jnp.broadcast_to(parts[b][0][:, start + i : start + i + 1], (8, 128)) for b in range(i // 8, blocks)}
        for i in range(STEP)
    ]
    scale = [jnp.ones((8, 128), f32) for b in range(blocks)]
    for k in range(STEP):
        at, ks = k // 8, k % 8
        pivot = spread(cols[k][at], ks)
        inverse = 1.0 / pivot
        factor = {b: cols[k][b] * inverse for b in range(at, blocks)}
        scale[at] = jnp.where(sub == ks, lax.rsqrt(pivot), scale[at])
        for i in range(k + 1, STEP):
            beside = spread(cols[k][i // 8], i % 8)
            for b in range(i // 8, blocks):
                cols[i][b] = cols[i][b] - factor[b] * beside
        factor[at] = jnp.where(sub > ks, factor[at], 0.0)
        for t in range(2):
            row = spread(parts[at][t], ks)
            for b in range(at, blocks):
                parts[b][t] = parts[b][t] - factor[b] * row
    return jnp.concatenate(
        [jnp.concatenate([parts[b][t] * scale[b] for t in range(2)], axis=1) for b in range(blocks)], axis=0
    )


def factor_diag(work, rows):
    for start in range(0, 128, STEP):
        after = start + STEP
        done = pivots(work, start)
        rows[start:after, :] = done
        if after < 128:
            change = dot_tn(triple(done[:, :128], "hhl", 0), triple(done, "hlh", 0))
            work[after:128, :] = work[after:128, :] - change[after:128, :]


def factor_kernel(place, own, other, hankel, upper, basis, gram, work, rows, behind):
    core = place[1]
    for source, half in ((own, core), (other, 1 - core)):
        for t in range(2 * OWNERS + GROUPS):
            (i, j), s = PAIRS[t // 8], t % 8
            if t < 2 * OWNERS:
                value = source[t // 2, 8 * (t % 2) : 8 * (t % 2) + 8, :]
            else:
                m = 2 * (t - 2 * OWNERS)
                value = jnp.concatenate([source[m, 16:20, :], source[m + 1, 16:20, :]], axis=0)
            at = pl.multiple_of(CHANNELS * i + HALF * half + 8 * s, 8)
            gram[pl.ds(at, 8), CHANNELS * j : CHANNELS * (j + 1)] = value * (1.0 / TOTAL)
    above = lax.broadcasted_iota(jnp.int32, (128, 128), 1)
    below = lax.broadcasted_iota(jnp.int32, (128, 128), 0)
    for p in range(4):
        lo, hi = 128 * p, 128 * p + 128
        work[:, 0:128] = gram[lo:hi, lo:hi]
        work[:, 128:256] = (above == below).astype(f32)
        factor_diag(work, rows)
        upper[lo:hi, lo:hi] = jnp.where(above >= below, rows[:, 0:128], 0.0)
        if p > 0:
            upper[lo:hi, 0:lo] = jnp.zeros((128, lo), f32)
        inverse = jnp.where(above <= below, rows[:, 128:256], 0.0)
        stacked = triple(inverse, "hhl", 1)
        if p > 0:
            left = dot_nn(stacked, triple(behind[lo:hi, 0:lo], "hlh", 0))
            full = jnp.concatenate([left, inverse], axis=1)
        else:
            full = inverse
        if p < 3:
            right = dot_nn(stacked, triple(gram[lo:hi, hi:512], "hlh", 0))
            upper[lo:hi, hi:512] = right
            first, second = triple(right, "hhl", 0), triple(right, "hlh", 0)
            for q in range(p + 1, 4):
                a = 128 * (q - p - 1)
                at = slice(128 * q, 128 * q + 128), slice(128 * q, 512)
                gram[at] = gram[at] - dot_tn(first[:, a : a + 128], second[:, a:])
            change = dot_tn(first, triple(full, "hlh", 0))
            if p > 0:
                behind[hi:512, 0:lo] = behind[hi:512, 0:lo] - change[:, 0:lo]
            behind[hi:512, lo:hi] = -change[:, lo:hi]
        high, low = split(full)
        basis[:, lo:hi] = (dot_nt(hankel[:, 0:hi], high) + dot_nt(hankel[:, 0:hi], low)).astype(bf16)


def factor(place, own, other, hankel):
    return pl.pallas_call(
        factor_kernel,
        out_shape=(jax.ShapeDtypeStruct((COLS, COLS), f32), jax.ShapeDtypeStruct((ROWS, COLS), bf16)),
        in_specs=[SMEM, VMEM, VMEM, VMEM],
        scratch_shapes=[
            pltpu.VMEM((COLS, COLS), f32),
            pltpu.VMEM((128, 256), f32),
            pltpu.VMEM((128, 256), f32),
            pltpu.VMEM((COLS, 384), f32),
        ],
        compiler_params=PARAMS,
        name="factor",
    )(place, own, other, hankel)


def shards(records, dropout, counts):
    core = lax.axis_index("core")
    place = jnp.stack([2 * lax.axis_index("zh") + lax.axis_index("zl"), core]).astype(jnp.int32)
    recs, drops = records.T, dropout.T
    head = (recs[:, :128].astype(f32) * drops[:, :128].astype(f32)).astype(bf16)
    head = lax.ppermute(head, GRP, [(g, g - 1) for g in range(1, GROUPS)])
    sent = pl.pallas_call(
        pack_kernel,
        out_shape=jax.ShapeDtypeStruct((32, 4, WINDOW), bf16),
        in_specs=[SMEM, SMEM, VMEM, VMEM],
        compiler_params=PARAMS,
        cost_estimate=pl.CostEstimate(flops=10**5, bytes_accessed=10**6, transcendentals=0),
        name="pack",
    )(place, counts, recs, drops)
    sent = pl.pallas_call(
        head_kernel,
        out_shape=jax.ShapeDtypeStruct((32, 4, WINDOW), bf16),
        in_specs=[SMEM, VMEM, ANY],
        out_specs=ANY,
        input_output_aliases={2: 0},
        scratch_shapes=[pltpu.VMEM((2, 4, 128), bf16), pltpu.SemaphoreType.DMA],
        compiler_params=PARAMS,
        name="add_head",
    )(counts, head, sent)
    series = lax.all_to_all(sent, DEV, 0, 0, tiled=True).reshape(CHANNELS, WINDOW)
    packed, hankel = pl.pallas_call(
        gram_kernel,
        out_shape=(jax.ShapeDtypeStruct((OWNERS, SLICE, 128), f32), jax.ShapeDtypeStruct((ROWS, COLS), bf16)),
        in_specs=[SMEM, VMEM],
        scratch_shapes=[pltpu.VMEM((COLS, 512), bf16)],
        compiler_params=PARAMS,
        name="partial_gram",
    )(place, series)
    parts = lax.all_to_all(packed, OWNER, 0, 0, tiled=True)
    parts = lax.all_to_all(add_up(parts, PLANES), "zh", 0, 0, tiled=True)
    own = lax.all_to_all(add_up(parts, OWNERS), OWNER, 0, 0, tiled=True)
    other = lax.ppermute(own, "core", [(0, 1), (1, 0)])
    return factor(place, own, other, hankel)


GRP, DEV, OWNER = ("x", "y"), ("zh", "zl", "core"), ("x", "y", "zl")


def solution(mesh):
    fine = Mesh(mesh.devices.reshape(4, 4, PLANES, 2, 2), ("x", "y", "zh", "zl", "core"))
    in_specs = (P(GRP, DEV), P(GRP, DEV), P(GRP + DEV))
    out_specs = (P(), P(GRP + DEV, None))
    return jax.shard_map(shards, mesh=fine, in_specs=in_specs, out_specs=out_specs, check_vma=False)
```

```python
import jax
import jax.numpy as jnp
from jax import lax
from jax.experimental import pallas as pl
from jax.experimental.pallas import tpu as pltpu
from jax.sharding import Mesh
from jax.sharding import PartitionSpec as P

f32, bf16 = jnp.float32, jnp.bfloat16

LAGS = 4
CHANNELS = 128
ROWS = 256
COLS = 512
TOTAL = 131072
GROUPS = 16
OWNERS = 32
PLANES = 8
WINDOW = 640
PAIRS = [(i, j) for i in range(LAGS) for j in range(i, LAGS)]
HALF = 64
SLICE = HALF * len(PAIRS) // OWNERS
TALL = SLICE + 4
EDGE = 48
INNER = 16
STEP = 32

PARAMS = pltpu.CompilerParams(vmem_limit_bytes=48 * 2**20)
SMEM = pl.BlockSpec(memory_space=pltpu.SMEM)
VMEM = pl.BlockSpec(memory_space=pltpu.VMEM)


def split(x):
    high = x.astype(bf16)
    return high, (x - high.astype(f32)).astype(bf16)


def dot_tn(left, right):
    return lax.dot_general(left, right, (((0,), (0,)), ((), ())), preferred_element_type=f32)


def dot_nt(left, right):
    return lax.dot_general(left, right, (((1,), (1,)), ((), ())), preferred_element_type=f32)


def dot_nn(left, right):
    return jnp.dot(left, right, preferred_element_type=f32)


def triple(x, order, axis):
    high, low = split(x)
    return jnp.concatenate([low if c == "l" else high for c in order], axis=axis)


def pack_kernel(place, count, records, dropout, out):
    signal = (records[...].astype(f32) * dropout[...].astype(f32)).astype(bf16)
    lane = lax.broadcasted_iota(jnp.int32, (4, 128), 1)
    counted = jnp.full((4, 128), count[0], jnp.int32).astype(f32)
    for z in range(16):
        behind = signal[:, 512 * z + 512 : 512 * z + 640] if z < 15 else jnp.zeros((4, 128), bf16)
        behind = jnp.where(lane == 127, counted, behind.astype(f32)).astype(bf16)
        for core in range(2):
            out[2 * z + core, :, 0:512] = signal[:, 512 * z : 512 * z + 512]
            out[2 * z + core, :, 512:640] = behind


def gram_kernel(place, series, packed, hankel, edge, lagged):
    z, core = place[0], place[1]
    samples = series[...].astype(f32)
    source = lax.broadcasted_iota(jnp.int32, (CHANNELS, 1), 0)
    tail = samples[:, WINDOW - 1 : WINDOW]
    time = lax.broadcasted_iota(jnp.int32, (1, 512), 1)
    counts = [
        jnp.sum(jnp.where(source == 8 * z + 4 * e, tail, 0.0), axis=0, keepdims=True) for e in range(2)
    ]
    least = jnp.where(time < ROWS, ROWS - counts[0], 2 * ROWS - counts[1])
    own_rows = jnp.where(z == 15, 2 * ROWS - 3, 2 * ROWS)
    valid = (time.astype(f32) >= least) & (time < own_rows)
    for i in range(LAGS):
        moved = samples if i == 0 else pltpu.roll(samples, WINDOW - i, 1)
        lagged[CHANNELS * i : CHANNELS * (i + 1), :] = jnp.where(valid, moved[:, :512], 0.0).astype(bf16)
    every = lagged[...]
    mine = jnp.concatenate(
        [lagged[pl.ds(pl.multiple_of(CHANNELS * i + HALF * core, HALF), HALF), :] for i in range(LAGS)], axis=0
    )
    gram = dot_nt(mine, every)

    def tile(t):
        (i, j), s = PAIRS[t // 8], t % 8
        return gram[HALF * i + 8 * s : HALF * i + 8 * s + 8, CHANNELS * j : CHANNELS * (j + 1)]

    for m in range(OWNERS):
        packed[m, 0:8, :] = tile(2 * m)
        packed[m, 8:16, :] = tile(2 * m + 1)
        packed[m, 16:20, :] = tile(2 * OWNERS + m // 2)[4 * (m % 2) : 4 * (m % 2) + 4, :]
    own = lagged[:, pl.ds(pl.multiple_of(ROWS * core, ROWS), ROWS)]
    hankel[...] = jnp.transpose(own.astype(f32)).astype(bf16)
    head = jnp.transpose(samples[:, 0:128])[0:8, :]
    tail = pltpu.roll(jnp.transpose(samples[:, 384:512])[120:128, :], 3, 0)
    used = lax.broadcasted_iota(jnp.int32, (8, 128), 0) < 3
    edge[...] = jnp.where(used & (z == 0), head, 0.0) + jnp.where(used & (z == 15), tail, 0.0)


def sum_edge_kernel(parts, edge, out):
    total = parts[0]
    for s in range(1, OWNERS):
        total = total + parts[s]
    for s in range(PLANES):
        out[s, 0:SLICE, :] = total
        out[s, SLICE:TALL, :] = edge[0:4, :]


def sum_kernel(parts, out):
    total = parts[0]
    for s in range(1, PLANES):
        total = total + parts[s]
    for s in range(OWNERS):
        out[s] = total


def spread(value, sublane):
    return jnp.broadcast_to(value[sublane : sublane + 1, :], (8, 128))


def pivots(work, start):
    sub = lax.broadcasted_iota(jnp.int32, (8, 128), 0)
    blocks = STEP // 8
    parts = [
        [work[start + 8 * b : start + 8 * b + 8, 128 * t : 128 * t + 128] for t in range(2)] for b in range(blocks)
    ]
    cols = {}
    scale = [jnp.ones((8, 128), f32) for b in range(blocks)]
    for k in range(STEP):
        at, ks = k // 8, k % 8
        if k % INNER == 0:
            for i in range(k, k + INNER):
                lane = start + i
                cols[i] = {b: jnp.broadcast_to(parts[b][0][:, lane : lane + 1], (8, 128)) for b in range(i // 8, blocks)}
        pivot = spread(cols[k][at], ks)
        inverse = 1.0 / pivot
        factor = {b: cols[k][b] * inverse for b in range(at, blocks)}
        scale[at] = jnp.where(sub == ks, lax.rsqrt(pivot), scale[at])
        for i in range(k + 1, k // INNER * INNER + INNER):
            beside = spread(cols[k][i // 8], i % 8)
            for b in range(i // 8, blocks):
                cols[i][b] = cols[i][b] - factor[b] * beside
        factor[at] = jnp.where(sub > ks, factor[at], 0.0)
        for t in range(2):
            row = spread(parts[at][t], ks)
            for b in range(at, blocks):
                parts[b][t] = parts[b][t] - factor[b] * row
    return jnp.concatenate(
        [jnp.concatenate([parts[b][t] * scale[b] for t in range(2)], axis=1) for b in range(blocks)], axis=0
    )


def factor_diag(work, rows):
    for start in range(0, 128, STEP):
        after = start + STEP
        done = pivots(work, start)
        rows[start:after, :] = done
        if after < 128:
            change = dot_tn(triple(done[:, :128], "hhl", 0), triple(done, "hlh", 0))
            work[after:128, :] = work[after:128, :] - change[after:128, :]


def edge_rows(own, samples):
    for m in range(OWNERS):
        samples[4 * m : 4 * m + 4, :] = own[m, SLICE:TALL, :]
    known = samples[...].astype(bf16)
    row = lax.broadcasted_iota(jnp.int32, (EDGE, 128), 0)
    source = lax.broadcasted_iota(jnp.int32, (EDGE, 128), 1)
    group = row % GROUPS
    lags = []
    for i in range(LAGS):
        ahead = row // GROUPS + i
        inside = (ahead < 3) & (source == 8 * group + 4 + ahead)
        outside = (ahead >= 3) & (group < GROUPS - 1) & (source == 8 * group + 8 + ahead - 3)
        lags.append(dot_nn((inside | outside).astype(f32).astype(bf16), known))
    return jnp.concatenate(lags, axis=1).astype(bf16)


def factor_kernel(place, own, other, hankel_in, upper, basis, gram, work, rows, behind, samples, hankel):
    z, core, group = place[0], place[1], place[2]
    edges = edge_rows(own, samples)
    hankel[...] = hankel_in[...]
    row = lax.broadcasted_iota(jnp.int32, (16, EDGE), 0)
    taken = lax.broadcasted_iota(jnp.int32, (16, EDGE), 1)
    ends = (row >= 13) & (taken == GROUPS * (row - 13) + group) & (z == 15) & (core == 1)
    patch = dot_nn(ends.astype(f32).astype(bf16), edges)
    hankel[240:256, :] = (hankel_in[240:256, :].astype(f32) + patch).astype(bf16)
    for source, half in ((own, core), (other, 1 - core)):
        for t in range(2 * OWNERS + GROUPS):
            (i, j), s = PAIRS[t // 8], t % 8
            if t < 2 * OWNERS:
                value = source[t // 2, 8 * (t % 2) : 8 * (t % 2) + 8, :]
            else:
                m = 2 * (t - 2 * OWNERS)
                value = jnp.concatenate([source[m, 16:20, :], source[m + 1, 16:20, :]], axis=0)
            at = pl.multiple_of(CHANNELS * i + HALF * half + 8 * s, 8)
            gram[pl.ds(at, 8), CHANNELS * j : CHANNELS * (j + 1)] = value * (1.0 / TOTAL)
    for i in range(LAGS):
        at = slice(CHANNELS * i, CHANNELS * (i + 1)), slice(CHANNELS * i, COLS)
        gram[at] = gram[at] + dot_tn(edges[:, at[0]], edges[:, at[1]]) * (1.0 / TOTAL)
    above = lax.broadcasted_iota(jnp.int32, (128, 128), 1)
    below = lax.broadcasted_iota(jnp.int32, (128, 128), 0)
    for p in range(4):
        lo, hi = 128 * p, 128 * p + 128
        work[:, 0:128] = gram[lo:hi, lo:hi]
        work[:, 128:256] = (above == below).astype(f32)
        factor_diag(work, rows)
        upper[lo:hi, lo:hi] = jnp.where(above >= below, rows[:, 0:128], 0.0)
        if p > 0:
            upper[lo:hi, 0:lo] = jnp.zeros((128, lo), f32)
        inverse = jnp.where(above <= below, rows[:, 128:256], 0.0)
        stacked = triple(inverse, "hhl", 1)
        if p > 0:
            left = dot_nn(stacked, triple(behind[lo:hi, 0:lo], "hlh", 0))
            full = jnp.concatenate([left, inverse], axis=1)
        else:
            full = inverse
        if p < 3:
            right = dot_nn(stacked, triple(gram[lo:hi, hi:512], "hlh", 0))
            upper[lo:hi, hi:512] = right
            first, second = triple(right, "hhl", 0), triple(right, "hlh", 0)
            for q in range(p + 1, 4):
                a = 128 * (q - p - 1)
                at = slice(128 * q, 128 * q + 128), slice(128 * q, 512)
                gram[at] = gram[at] - dot_tn(first[:, a : a + 128], second[:, a:])
            change = dot_tn(first, triple(full, "hlh", 0))
            if p > 0:
                behind[hi:512, 0:lo] = behind[hi:512, 0:lo] - change[:, 0:lo]
            behind[hi:512, lo:hi] = -change[:, lo:hi]
        high, low = split(full)
        basis[:, lo:hi] = (dot_nt(hankel[:, 0:hi], high) + dot_nt(hankel[:, 0:hi], low)).astype(bf16)


def factor(place, own, other, hankel):
    return pl.pallas_call(
        factor_kernel,
        out_shape=(jax.ShapeDtypeStruct((COLS, COLS), f32), jax.ShapeDtypeStruct((ROWS, COLS), bf16)),
        in_specs=[SMEM, VMEM, VMEM, VMEM],
        scratch_shapes=[
            pltpu.VMEM((COLS, COLS), f32),
            pltpu.VMEM((128, 256), f32),
            pltpu.VMEM((128, 256), f32),
            pltpu.VMEM((COLS, 384), f32),
            pltpu.VMEM((4 * OWNERS, 128), f32),
            pltpu.VMEM((ROWS, COLS), bf16),
        ],
        compiler_params=PARAMS,
        name="factor",
    )(place, own, other, hankel)


def call(kernel, out_shape, in_specs, name, scratch=()):
    return pl.pallas_call(
        kernel, out_shape=out_shape, in_specs=in_specs, scratch_shapes=scratch, compiler_params=PARAMS, name=name
    )


def shards(records, dropout, counts):
    group = 4 * lax.axis_index("x") + lax.axis_index("y")
    z = 2 * lax.axis_index("zh") + lax.axis_index("zl")
    place = jnp.stack([z, lax.axis_index("core"), group]).astype(jnp.int32)
    sent = call(
        pack_kernel, jax.ShapeDtypeStruct((32, 4, WINDOW), bf16), [SMEM, SMEM, VMEM, VMEM], "pack"
    )(place, counts, records.T, dropout.T)
    series = lax.all_to_all(sent, DEV, 0, 0, tiled=True).reshape(CHANNELS, WINDOW)
    packed, hankel, edge = call(
        gram_kernel,
        (
            jax.ShapeDtypeStruct((OWNERS, SLICE, 128), f32),
            jax.ShapeDtypeStruct((ROWS, COLS), bf16),
            jax.ShapeDtypeStruct((8, 128), f32),
        ),
        [SMEM, VMEM],
        "partial_gram",
        [pltpu.VMEM((COLS, 512), bf16)],
    )(place, series)
    parts = lax.all_to_all(packed, OWNER, 0, 0, tiled=True)
    parts = call(sum_edge_kernel, jax.ShapeDtypeStruct((PLANES, TALL, 128), f32), [VMEM, VMEM], "add_owners")(parts, edge)
    parts = lax.all_to_all(parts, "zh", 0, 0, tiled=True)
    parts = call(sum_kernel, jax.ShapeDtypeStruct((OWNERS, TALL, 128), f32), [VMEM], "add_planes")(parts)
    own = lax.all_to_all(parts, OWNER, 0, 0, tiled=True)
    other = lax.ppermute(own, "core", [(0, 1), (1, 0)])
    return factor(place, own, other, hankel)


GRP, DEV, OWNER = ("x", "y"), ("zh", "zl", "core"), ("x", "y", "zl")


def solution(mesh):
    fine = Mesh(mesh.devices.reshape(4, 4, PLANES, 2, 2), ("x", "y", "zh", "zl", "core"))
    in_specs = (P(GRP, DEV), P(GRP, DEV), P(GRP + DEV))
    out_specs = (P(), P(GRP + DEV, None))
    return jax.shard_map(shards, mesh=fine, in_specs=in_specs, out_specs=out_specs, check_vma=False)
```

```python
import jax
import jax.numpy as jnp
from jax import lax
from jax.experimental import pallas as pl
from jax.experimental.pallas import tpu as pltpu
from jax.sharding import Mesh
from jax.sharding import PartitionSpec as P

f32, bf16 = jnp.float32, jnp.bfloat16

LAGS = 4
CHANNELS = 128
ROWS = 256
COLS = 512
TOTAL = 131072
GROUPS = 16
OWNERS = 32
PLANES = 8
WINDOW = 640
PAIRS = [(i, j) for i in range(LAGS) for j in range(i, LAGS)]
HALF = 64
SLICE = HALF * len(PAIRS) // OWNERS
TALL = SLICE + 4
EDGE = 48
INNER = 16
EARLY = 4
STEP = 32

PARAMS = pltpu.CompilerParams(vmem_limit_bytes=48 * 2**20)
SMEM = pl.BlockSpec(memory_space=pltpu.SMEM)
VMEM = pl.BlockSpec(memory_space=pltpu.VMEM)


def split(x):
    high = x.astype(bf16)
    return high, (x - high.astype(f32)).astype(bf16)


def dot_tn(left, right):
    return lax.dot_general(left, right, (((0,), (0,)), ((), ())), preferred_element_type=f32)


def dot_nt(left, right):
    return lax.dot_general(left, right, (((1,), (1,)), ((), ())), preferred_element_type=f32)


def dot_nn(left, right):
    return jnp.dot(left, right, preferred_element_type=f32)


def triple(x, order, axis):
    high, low = split(x)
    return jnp.concatenate([low if c == "l" else high for c in order], axis=axis)


def pack_kernel(place, count, records, dropout, out):
    signal = (records[...].astype(f32) * dropout[...].astype(f32)).astype(bf16)
    lane = lax.broadcasted_iota(jnp.int32, (4, 128), 1)
    counted = jnp.full((4, 128), count[0], jnp.int32).astype(f32)
    for z in range(16):
        behind = signal[:, 512 * z + 512 : 512 * z + 640] if z < 15 else jnp.zeros((4, 128), bf16)
        behind = jnp.where(lane == 127, counted, behind.astype(f32)).astype(bf16)
        for core in range(2):
            out[2 * z + core, :, 0:512] = signal[:, 512 * z : 512 * z + 512]
            out[2 * z + core, :, 512:640] = behind


def gram_kernel(place, series, packed, hankel, edge, lagged):
    z, core = place[0], place[1]
    samples = series[...].astype(f32)
    source = lax.broadcasted_iota(jnp.int32, (CHANNELS, 1), 0)
    tail = samples[:, WINDOW - 1 : WINDOW]
    time = lax.broadcasted_iota(jnp.int32, (1, 512), 1)
    counts = [
        jnp.sum(jnp.where(source == 8 * z + 4 * e, tail, 0.0), axis=0, keepdims=True) for e in range(2)
    ]
    least = jnp.where(time < ROWS, ROWS - counts[0], 2 * ROWS - counts[1])
    own_rows = jnp.where(z == 15, 2 * ROWS - 3, 2 * ROWS)
    valid = (time.astype(f32) >= least) & (time < own_rows)
    for i in range(LAGS):
        moved = samples if i == 0 else pltpu.roll(samples, WINDOW - i, 1)
        lagged[CHANNELS * i : CHANNELS * (i + 1), :] = jnp.where(valid, moved[:, :512], 0.0).astype(bf16)
    every = lagged[...]
    mine = jnp.concatenate(
        [lagged[pl.ds(pl.multiple_of(CHANNELS * i + HALF * core, HALF), HALF), :] for i in range(LAGS)], axis=0
    )
    gram = dot_nt(mine, every)

    def tile(t):
        (i, j), s = PAIRS[t // 8], t % 8
        return gram[HALF * i + 8 * s : HALF * i + 8 * s + 8, CHANNELS * j : CHANNELS * (j + 1)]

    for m in range(OWNERS):
        packed[m, 0:8, :] = tile(2 * m)
        packed[m, 8:16, :] = tile(2 * m + 1)
        packed[m, 16:20, :] = tile(2 * OWNERS + m // 2)[4 * (m % 2) : 4 * (m % 2) + 4, :]
    own = lagged[:, pl.ds(pl.multiple_of(ROWS * core, ROWS), ROWS)]
    hankel[...] = jnp.transpose(own.astype(f32)).astype(bf16)
    head = jnp.transpose(samples[:, 0:128])[0:8, :]
    tail = pltpu.roll(jnp.transpose(samples[:, 384:512])[120:128, :], 3, 0)
    used = lax.broadcasted_iota(jnp.int32, (8, 128), 0) < 3
    edge[...] = jnp.where(used & (z == 0), head, 0.0) + jnp.where(used & (z == 15), tail, 0.0)


def sum_edge_kernel(parts, edge, out):
    total = parts[0]
    for s in range(1, OWNERS):
        total = total + parts[s]
    for s in range(PLANES):
        out[s, 0:SLICE, :] = total
        out[s, SLICE:TALL, :] = edge[0:4, :]


def sum_kernel(parts, out):
    total = parts[0]
    for s in range(1, PLANES):
        total = total + parts[s]
    for s in range(OWNERS):
        out[s] = total


def spread(value, sublane):
    return jnp.broadcast_to(value[sublane : sublane + 1, :], (8, 128))


def pivots(work, start):
    sub = lax.broadcasted_iota(jnp.int32, (8, 128), 0)
    lane = lax.broadcasted_iota(jnp.int32, (8, 128), 1)
    blocks = STEP // 8
    parts = [work[start + 8 * b : start + 8 * b + 8, :] for b in range(blocks)]
    cols = {}
    scale = [jnp.ones((8, 128), f32) for b in range(blocks)]
    for k in range(0, STEP, 2):
        at, ks = k // 8, k % 8
        if k == 0 or k % INNER == INNER - EARLY:
            for i in range(len(cols), min(len(cols) + INNER, STEP)):
                c = start + i
                cols[i] = {b: jnp.broadcast_to(parts[b][:, c : c + 1], (8, 128)) for b in range(i // 8, blocks)}
        one, two = cols[k], cols[k + 1]
        first, cross, second = spread(one[at], ks), spread(one[at], ks + 1), spread(two[at], ks + 1)
        det = first * second - cross * cross
        inverse = 1.0 / det
        ratio = 1.0 / first
        below = range(at, blocks)
        u = {b: second * one[b] - cross * two[b] for b in below}
        v = {b: first * two[b] - cross * one[b] for b in below}
        us = {b: u[b] * inverse for b in below}
        vs = {b: v[b] * inverse for b in below}
        for i in range(k + 2, len(cols)):
            left, right = spread(one[i // 8], i % 8), spread(two[i // 8], i % 8)
            for b in range(i // 8, blocks):
                if i < k + 4:
                    cols[i][b] = cols[i][b] - (u[b] * left + v[b] * right) * inverse
                else:
                    cols[i][b] = cols[i][b] - (us[b] * left + vs[b] * right)
        scale[at] = jnp.where(sub == ks, lax.rsqrt(first), scale[at])
        scale[at] = jnp.where(sub == ks + 1, lax.rsqrt(det * ratio), scale[at])
        us[at] = jnp.where(sub > ks + 1, us[at], jnp.where(sub == ks + 1, cross * ratio, 0.0))
        vs[at] = jnp.where(sub > ks + 1, vs[at], 0.0)
        here, next_to = lane == start + k, lane == start + k + 1
        left = jnp.where(here, 1.0, jnp.where(next_to, 0.0, spread(parts[at], ks)))
        right = jnp.where(here, 0.0, jnp.where(next_to, 1.0, spread(parts[at], ks + 1)))
        fresh = (here & (sub >= ks)) | (next_to & (sub >= ks + 1))
        unit = (here & (sub == ks)) | (next_to & (sub == ks + 1))
        parts[at] = jnp.where(fresh, unit.astype(f32), parts[at]) - (us[at] * left + vs[at] * right)
        for b in range(at + 1, blocks):
            parts[b] = jnp.where(here | next_to, 0.0, parts[b]) - (us[b] * left + vs[b] * right)
    return jnp.concatenate([parts[b] * scale[b] for b in range(blocks)], axis=0)


def factor_diag(work, rows):
    row = lax.broadcasted_iota(jnp.int32, (STEP, 128), 0)
    lane = lax.broadcasted_iota(jnp.int32, (STEP, 128), 1)
    for start in range(0, 128, STEP):
        after = start + STEP
        done = pivots(work, start)
        rows[start:after, :] = done
        if after < 128:
            right = jnp.where((lane < after) & (lane > start + row), 0.0, done)
            change = dot_tn(triple(done, "hhl", 0), triple(right, "hlh", 0))
            group = lax.broadcasted_iota(jnp.int32, (128 - after, 128), 1)
            group = (group >= start) & (group < after)
            work[after:128, :] = jnp.where(group, 0.0, work[after:128, :]) - change[after:128, :]


def edge_rows(own, samples):
    for m in range(OWNERS):
        samples[4 * m : 4 * m + 4, :] = own[m, SLICE:TALL, :]
    known = samples[...].astype(bf16)
    row = lax.broadcasted_iota(jnp.int32, (EDGE, 128), 0)
    source = lax.broadcasted_iota(jnp.int32, (EDGE, 128), 1)
    group = row % GROUPS
    lags = []
    for i in range(LAGS):
        ahead = row // GROUPS + i
        inside = (ahead < 3) & (source == 8 * group + 4 + ahead)
        outside = (ahead >= 3) & (group < GROUPS - 1) & (source == 8 * group + 8 + ahead - 3)
        lags.append(dot_nn((inside | outside).astype(f32).astype(bf16), known))
    return jnp.concatenate(lags, axis=1).astype(bf16)


def factor_kernel(place, own, other, hankel_in, upper, basis, gram, work, rows, behind, samples, hankel):
    z, core, group = place[0], place[1], place[2]
    edges = edge_rows(own, samples)
    hankel[...] = hankel_in[...]
    row = lax.broadcasted_iota(jnp.int32, (16, EDGE), 0)
    taken = lax.broadcasted_iota(jnp.int32, (16, EDGE), 1)
    ends = (row >= 13) & (taken == GROUPS * (row - 13) + group) & (z == 15) & (core == 1)
    patch = dot_nn(ends.astype(f32).astype(bf16), edges)
    hankel[240:256, :] = (hankel_in[240:256, :].astype(f32) + patch).astype(bf16)
    for source, half in ((own, core), (other, 1 - core)):
        for t in range(2 * OWNERS + GROUPS):
            (i, j), s = PAIRS[t // 8], t % 8
            if t < 2 * OWNERS:
                value = source[t // 2, 8 * (t % 2) : 8 * (t % 2) + 8, :]
            else:
                m = 2 * (t - 2 * OWNERS)
                value = jnp.concatenate([source[m, 16:20, :], source[m + 1, 16:20, :]], axis=0)
            at = pl.multiple_of(CHANNELS * i + HALF * half + 8 * s, 8)
            gram[pl.ds(at, 8), CHANNELS * j : CHANNELS * (j + 1)] = value * (1.0 / TOTAL)
    for i in range(LAGS):
        at = slice(CHANNELS * i, CHANNELS * (i + 1)), slice(CHANNELS * i, COLS)
        gram[at] = gram[at] + dot_tn(edges[:, at[0]], edges[:, at[1]]) * (1.0 / TOTAL)
    above = lax.broadcasted_iota(jnp.int32, (128, 128), 1)
    below = lax.broadcasted_iota(jnp.int32, (128, 128), 0)
    diagonals = [jnp.where(above == below, gram[128 * p : 128 * p + 128, 128 * p : 128 * p + 128], 0.0) for p in range(4)]
    inward = [lax.rsqrt(jnp.sum(d, axis=0, keepdims=True)) for d in diagonals]
    outward = [1.0 / v for v in inward]
    for p in range(4):
        rows_in = lax.rsqrt(jnp.sum(diagonals[p], axis=1, keepdims=True))
        for q in range(p, 4):
            at = slice(128 * p, 128 * p + 128), slice(128 * q, 128 * q + 128)
            gram[at] = gram[at] * rows_in * inward[q]
    for p in range(4):
        lo, hi = 128 * p, 128 * p + 128
        work[...] = gram[lo:hi, lo:hi]
        factor_diag(work, rows)
        both = rows[...]
        upper[lo:hi, lo:hi] = jnp.where(above > below, both, jnp.where(above == below, 1.0 / both, 0.0)) * outward[p]
        if p > 0:
            upper[lo:hi, 0:lo] = jnp.zeros((128, lo), f32)
        inverse = jnp.where(above <= below, both, 0.0)
        stacked = triple(inverse, "hhl", 1)
        if p > 0:
            left = dot_nn(stacked, triple(behind[lo:hi, 0:lo], "hlh", 0))
            full = jnp.concatenate([left, inverse], axis=1)
        else:
            full = inverse
        if p < 3:
            right = dot_nn(stacked, triple(gram[lo:hi, hi:512], "hlh", 0))
            upper[lo:hi, hi:512] = right * jnp.concatenate(outward[p + 1 :], axis=1)
            first, second = triple(right, "hhl", 0), triple(right, "hlh", 0)
            for q in range(p + 1, 4):
                a = 128 * (q - p - 1)
                at = slice(128 * q, 128 * q + 128), slice(128 * q, 512)
                gram[at] = gram[at] - dot_tn(first[:, a : a + 128], second[:, a:])
            change = dot_tn(first, triple(full, "hlh", 0))
            if p > 0:
                behind[hi:512, 0:lo] = behind[hi:512, 0:lo] - change[:, 0:lo]
            behind[hi:512, lo:hi] = -change[:, lo:hi]
        high, low = split(full * jnp.concatenate(inward[: p + 1], axis=1))
        basis[:, lo:hi] = (dot_nt(hankel[:, 0:hi], high) + dot_nt(hankel[:, 0:hi], low)).astype(bf16)


def factor(place, own, other, hankel):
    return pl.pallas_call(
        factor_kernel,
        out_shape=(jax.ShapeDtypeStruct((COLS, COLS), f32), jax.ShapeDtypeStruct((ROWS, COLS), bf16)),
        in_specs=[SMEM, VMEM, VMEM, VMEM],
        scratch_shapes=[
            pltpu.VMEM((COLS, COLS), f32),
            pltpu.VMEM((128, 128), f32),
            pltpu.VMEM((128, 128), f32),
            pltpu.VMEM((COLS, 384), f32),
            pltpu.VMEM((4 * OWNERS, 128), f32),
            pltpu.VMEM((ROWS, COLS), bf16),
        ],
        compiler_params=PARAMS,
        name="factor",
    )(place, own, other, hankel)


def call(kernel, out_shape, in_specs, name, scratch=()):
    return pl.pallas_call(
        kernel, out_shape=out_shape, in_specs=in_specs, scratch_shapes=scratch, compiler_params=PARAMS, name=name
    )


def shards(records, dropout, counts):
    group = 4 * lax.axis_index("x") + lax.axis_index("y")
    z = 2 * lax.axis_index("zh") + lax.axis_index("zl")
    place = jnp.stack([z, lax.axis_index("core"), group]).astype(jnp.int32)
    sent = call(
        pack_kernel, jax.ShapeDtypeStruct((32, 4, WINDOW), bf16), [SMEM, SMEM, VMEM, VMEM], "pack"
    )(place, counts, records.T, dropout.T)
    series = lax.all_to_all(sent, DEV, 0, 0, tiled=True).reshape(CHANNELS, WINDOW)
    packed, hankel, edge = call(
        gram_kernel,
        (
            jax.ShapeDtypeStruct((OWNERS, SLICE, 128), f32),
            jax.ShapeDtypeStruct((ROWS, COLS), bf16),
            jax.ShapeDtypeStruct((8, 128), f32),
        ),
        [SMEM, VMEM],
        "partial_gram",
        [pltpu.VMEM((COLS, 512), bf16)],
    )(place, series)
    parts = lax.all_to_all(packed, OWNER, 0, 0, tiled=True)
    parts = call(sum_edge_kernel, jax.ShapeDtypeStruct((PLANES, TALL, 128), f32), [VMEM, VMEM], "add_owners")(parts, edge)
    parts = lax.all_to_all(parts, "zh", 0, 0, tiled=True)
    parts = call(sum_kernel, jax.ShapeDtypeStruct((OWNERS, TALL, 128), f32), [VMEM], "add_planes")(parts)
    own = lax.all_to_all(parts, OWNER, 0, 0, tiled=True)
    other = lax.ppermute(own, "core", [(0, 1), (1, 0)])
    return factor(place, own, other, hankel)


GRP, DEV, OWNER = ("x", "y"), ("zh", "zl", "core"), ("x", "y", "zl")


def solution(mesh):
    fine = Mesh(mesh.devices.reshape(4, 4, PLANES, 2, 2), ("x", "y", "zh", "zl", "core"))
    in_specs = (P(GRP, DEV), P(GRP, DEV), P(GRP + DEV))
    out_specs = (P(), P(GRP + DEV, None))
    return jax.shard_map(shards, mesh=fine, in_specs=in_specs, out_specs=out_specs, check_vma=False)
```
